256 devices in a mesh: inner: 32 (over y, z_hi, core), outer: 8 (over z_lo, x).
Axes of the slice: x: 4, y: 4, z: 8 (z_hi: 4, z_lo: 2; z = z_hi * 2 + z_lo), core: 2. Of those that a mesh axis runs over, the one named last changes fastest.
Arguments:
- tokens: bfloat16 [65536, 8192], P(('inner', 'outer')), may hold values from -24 to 24
- grad_out: bfloat16 [65536, 8192], P(('inner', 'outer')), may hold values from -0.09375 to 0.09375
- gate_rows: bfloat16 [104, 8192], replicated, may hold values from -0.0625 to 0.0625
- up_rows: bfloat16 [104, 8192], replicated, may hold values from -0.0625 to 0.0625
- down_rows: bfloat16 [104, 8192], replicated, may hold values from -0.0390625 to 0.0390625
Outputs:
- grad_blocks: float32 [3, 3328, 256], P(None, ('inner', 'outer'))
The draws below stay inside these ranges and needn't reach their ends.
All inputs are finite; a program needn't handle non-finite values. Where the reference program divides by a largest or mean magnitude, that divisor is 1e-20 or more.
Results may differ from the reference program's by a relative error of at most 0.0095.
Values may be sent and summed in bfloat16 or wider, within the bound.
No kernel may reach another device: no remote copies, remote signals or barrier semaphores. Data moves between devices by JAX's collectives and lax.ppermute only.
A program may use at most 128 MiB of HBM per device.

```python
import jax
import jax.numpy as jnp
from jax import lax

D = 8192
FF = 22016
BUCKET = 104
BLOCK = 256
TOK_DEV = 256
TOKENS = 65536
NBM = 3328
N_INNER = 32
N_OUTER = 8


def raised(values, key, source, target, shards_of, factor):
    owner, partner = [(jnp.arange(values.shape[position]) // (values.shape[position] // shards_of)).reshape([-1 if axis == position else 1 for axis in range(values.ndim)]) for position in (source, target)]
    chosen = jax.random.permutation(key, shards_of)[partner]
    strong = (owner == chosen) | (owner == (partner + shards_of // 2) % shards_of)
    return jnp.where(strong, factor * values, values)


def levels(key, shape, shards, smallest, largest):
    def one(axis_at, blocks):
        heights = jax.random.uniform(jax.random.fold_in(jax.random.fold_in(key, 6), axis_at), (blocks,), jnp.float32, smallest / len(shards), largest / len(shards))
        return jnp.repeat(jnp.exp(heights), shape[axis_at] // blocks).reshape((-1,) + (1,) * (len(shape) - axis_at - 1))

    gain = one(*shards[0])
    for cut in shards[1:]:
        gain = gain * one(*cut)
    return gain


def bell_draw(stream_key, extent, scale, reach, cuts=(), held_as=jnp.bfloat16):
    drawn = jax.random.normal(stream_key, extent, jnp.float32) * scale
    if len(cuts) > 0:
        drawn = levels(stream_key, extent, cuts, -0.22, 0.18) * drawn
    return jnp.clip(drawn, min=-reach, max=reach).astype(held_as)


def bell_draw_with(own_key, extent, scale, bound, split, heavy, held_as=jnp.bfloat16):
    values = scale * jax.random.normal(own_key, extent, jnp.float32)
    if split:
        values = values * levels(own_key, extent, split, -0.22, 0.18)
    return jnp.clip(raised(values, jax.random.fold_in(own_key, 3), *heavy), -bound, bound).astype(held_as)


def setup_inputs(seed: int = 0) -> dict:
    key_of = jax.random.split(jax.random.key(seed), 6)
    return {
        "tokens": bell_draw_with(key_of[0], (TOKENS, D), 1.0, 24.0, ((0, 256),), (0, 1, 256, 6.0)),
        "grad_out": bell_draw_with(key_of[1], (TOKENS, D), (TOKENS ** -0.5), 0.09375, ((0, 256),), (0, 1, 256, 6.0)),
        "gate_rows": bell_draw(key_of[2], (BUCKET, D), D ** -0.5, 0.0625),
        "up_rows": bell_draw(key_of[3], (BUCKET, D), D ** -0.5, 0.0625),
        "down_rows": bell_draw(key_of[4], (BUCKET, D), FF ** -0.5, 0.0390625),
    }


EPS = 1e-6


def encode_decode(values):
    scale = jnp.max(jnp.abs(values), axis=-1) + EPS
    codes = lax.optimization_barrier((values / scale[..., None]).astype(jnp.bfloat16))
    return codes.astype(jnp.float32) * scale[..., None]


def device_terms(rows_in, rows_grad, gate_rows, up_rows, down_rows):
    gate = jnp.dot(rows_in, gate_rows.T, preferred_element_type=jnp.float32)
    up = jnp.dot(rows_in, up_rows.T, preferred_element_type=jnp.float32)
    sig = jax.nn.sigmoid(gate)
    act = gate * sig
    hidden = (act * up).astype(jnp.bfloat16)
    dh = jnp.dot(rows_grad, down_rows.T, preferred_element_type=jnp.float32)
    dgate = (dh * up * sig * (1.0 + gate * (1.0 - sig))).astype(jnp.bfloat16)
    dup = (dh * act).astype(jnp.bfloat16)
    g_down = jnp.dot(hidden.T, rows_grad, preferred_element_type=jnp.float32)
    g_gate = jnp.dot(dgate.T, rows_in, preferred_element_type=jnp.float32)
    g_up = jnp.dot(dup.T, rows_in, preferred_element_type=jnp.float32)
    return jnp.stack([g_down, g_gate, g_up]).reshape(3, NBM, BLOCK)


def reference(tokens, grad_out, gate_rows, up_rows, down_rows):
    def step(totals, index):
        start = (index * TOK_DEV).astype(jnp.int32)
        rows_in = lax.dynamic_slice_in_dim(tokens, start, TOK_DEV, 0)
        rows_grad = lax.dynamic_slice_in_dim(grad_out, start, TOK_DEV, 0)
        term = encode_decode(device_terms(rows_in, rows_grad, gate_rows, up_rows, down_rows))
        return totals + term, None

    start_totals = jnp.zeros((3, NBM, BLOCK), jnp.float32)
    totals, _ = lax.scan(step, start_totals, jnp.arange(N_INNER * N_OUTER, dtype=jnp.int32))
    return totals
```

```python
import jax
import jax.numpy as jnp
from jax import lax
from jax.experimental import pallas as pl
from jax.experimental.pallas import tpu as pltpu
from jax.sharding import Mesh, PartitionSpec as P

ROWS = 104
D = 8192
BLK = 256
TOK = 256
NCB = D // BLK
OWN = 13
NR0 = 13
QUART = 104
CHUNK = 1024
NCH = D // CHUNK
PACK = 80
AXES = ("y", "zh", "c", "zl", "x")
F32 = jnp.float32
BF16 = jnp.bfloat16
VM = pl.BlockSpec(memory_space=pltpu.VMEM)
HB = pl.BlockSpec(memory_space=pltpu.HBM)
SM = pl.BlockSpec(memory_space=pltpu.SMEM)


def params(mib):
    return pltpu.CompilerParams(vmem_limit_bytes=mib * 1024 * 1024)


def shape(*dims, dtype=BF16):
    return jax.ShapeDtypeStruct(dims, dtype)


def weight_grads(core, a_ref, v_ref, nm, send_ref, own_ref):
    for mine in range(2):

        @pl.when(core == mine)
        def _(mine=mine):
            for cb in range(NCB):
                res = jnp.dot(a_ref[...], v_ref[:, cb * BLK : (cb + 1) * BLK], preferred_element_type=F32)
                for r0 in range(NR0):
                    quarter, off = divmod(NCB * r0 + cb, QUART)
                    out = own_ref if quarter % 2 == mine else send_ref
                    for m in range(nm):
                        lo = m * ROWS + 8 * r0
                        out[m, QUART * (quarter // 2) + off] = res[lo : lo + 8, :].astype(BF16)


def first_kernel(c_ref, x_hbm, g_hbm, wg_hbm, wu_hbm, wd_hbm, send_hbm, own_hbm, h_ref, *scratch):
    x_ref, g_ref, wg_ref, wu_ref, wd_ref, rows, tmp, a_ref, send, own, sems, out_sems = scratch
    copies = []
    pairs = ((x_hbm, x_ref), (wg_hbm, wg_ref), (wu_hbm, wu_ref), (g_hbm, g_ref), (wd_hbm, wd_ref))
    for i in range(NCH):
        cols = pl.ds(i * CHUNK, CHUNK)
        for k, (src, dst) in enumerate(pairs):
            copies.append(pltpu.make_async_copy(src.at[:, cols], dst.at[:, cols], sems.at[k, i]))
            copies[-1].start()

    def project(v, w):
        return lax.dot_general(v, w, (((1,), (1,)), ((), ())), preferred_element_type=F32)

    gate_up = jnp.zeros((TOK, 2 * ROWS), F32)
    back = jnp.zeros((TOK, ROWS), F32)
    for i in range(NCH):
        for k in range(5):
            copies[5 * i + k].wait()
        cols = slice(i * CHUNK, (i + 1) * CHUNK)
        both = jnp.concatenate([wg_ref[:, cols], wu_ref[:, cols]], axis=0)
        gate_up = gate_up + project(x_ref[:, cols], both)
        back = back + project(g_ref[:, cols], wd_ref[:, cols])
    gate_up = gate_up.T
    gate, up, dh = gate_up[:ROWS], gate_up[ROWS:], back.T
    sig = jax.nn.sigmoid(gate)
    act = gate * sig
    terms = (act * up, dh * up * sig * (1.0 + gate * (1.0 - sig)), dh * act)
    for i, term in enumerate(terms):
        for half in range(2):
            lanes = slice(128 * half, 128 * (half + 1))
            rows[i, half] = term[:, lanes]
            for r0 in range(NR0):
                tmp[i, 8 * r0 : 8 * (r0 + 1), lanes] = rows[i, half, pl.ds(r0, 8, stride=NR0), :]
    h_ref[...] = tmp[0].astype(BF16)
    a_ref[...] = jnp.concatenate([tmp[1], tmp[2]], axis=0).astype(BF16)
    weight_grads(c_ref[0], a_ref, x_ref, 2, send, own)
    write_out((send, send_hbm), (own, own_hbm), out_sems)


def write_out(one, two, sems):
    copies = [pltpu.make_async_copy(src, dst, sems.at[i]) for i, (src, dst) in enumerate((one, two))]
    for copy in copies:
        copy.start()
    for copy in copies:
        copy.wait()


def first(core, x, g, wg, wu, wd):
    half = (2, 2 * QUART, 8, BLK)
    return pl.pallas_call(
        first_kernel,
        in_specs=[SM, HB, HB, HB, HB, HB],
        out_specs=[HB, HB, VM],
        out_shape=[shape(*half), shape(*half), shape(ROWS, TOK)],
        scratch_shapes=[
            pltpu.VMEM((TOK, D), BF16),
            pltpu.VMEM((TOK, D), BF16),
            pltpu.VMEM((ROWS, D), BF16),
            pltpu.VMEM((ROWS, D), BF16),
            pltpu.VMEM((ROWS, D), BF16),
            pltpu.VMEM((3, 2, ROWS, 128), F32),
            pltpu.VMEM((3, ROWS, TOK), F32),
            pltpu.VMEM((2 * ROWS, TOK), BF16),
            pltpu.VMEM(half, BF16),
            pltpu.VMEM(half, BF16),
            pltpu.SemaphoreType.DMA((5, NCH)),
            pltpu.SemaphoreType.DMA((2,)),
        ],
        compiler_params=params(60),
        name="first",
    )(core, x, g, wg, wu, wd)


def down_kernel(c_ref, a_ref, g_hbm, send_hbm, own_hbm, g_ref, send, own, sems, out_sems):
    copies = []
    for i in range(NCH):
        cols = pl.ds(i * CHUNK, CHUNK)
        copies.append(pltpu.make_async_copy(g_hbm.at[:, cols], g_ref.at[:, cols], sems.at[i]))
        copies[-1].start()
    for copy in copies:
        copy.wait()
    weight_grads(c_ref[0], a_ref, g_ref, 1, send, own)
    write_out((send, send_hbm), (own, own_hbm), out_sems)


def down(core, a, g):
    half = (1, 2 * QUART, 8, BLK)
    return pl.pallas_call(
        down_kernel,
        in_specs=[SM, VM, HB],
        out_specs=[HB, HB],
        out_shape=[shape(*half), shape(*half)],
        scratch_shapes=[
            pltpu.VMEM((TOK, D), BF16),
            pltpu.VMEM(half, BF16),
            pltpu.VMEM(half, BF16),
            pltpu.SemaphoreType.DMA((NCH,)),
            pltpu.SemaphoreType.DMA((2,)),
        ],
        compiler_params=params(60),
        name="down",
    )(core, a, g)


def add_kernel(o0, g0, o1, g1, out_ref, packed):
    pairs = ((o0, g0, 0), (o1, g1, 0), (o1, g1, 1))
    for d in range(8):
        for t in range(8):
            for half in range(2):
                packed[half, d, PACK * t + 6 * OWN : PACK * (t + 1), :] = jnp.zeros((PACK - 6 * OWN, 128), F32)
        for m, (own, got, i) in enumerate(pairs):
            for low in range(2):
                for off in range(OWN):
                    at = QUART * low + OWN * d + off
                    tile = own[i, at].astype(F32) + got[i, at].astype(F32)
                    lo = OWN * (2 * m + low) + off
                    for half in range(2):
                        packed[half, d, pl.ds(lo, 8, stride=PACK), :] = tile[:, 128 * half : 128 * (half + 1)]
        for y in range(4):
            for half in range(2):
                piece = packed[half, d, 2 * PACK * y : 2 * PACK * (y + 1), :]
                out_ref[8 * y + d, :, 128 * half : 128 * (half + 1)] = piece.astype(BF16)


def add_cores(o0, g0, o1, g1):
    return pl.pallas_call(
        add_kernel,
        in_specs=[VM] * 4,
        out_specs=VM,
        out_shape=shape(32, 2 * PACK, BLK),
        scratch_shapes=[pltpu.VMEM((2, 8, 8 * PACK, 128), F32)],
        compiler_params=params(24),
        name="add_cores",
    )(o0, g0, o1, g1)


def sum_near_kernel(in_ref, out_ref, total, packed):
    total[...] = jnp.sum(in_ref[...].astype(F32), axis=0)
    packed[:, 3 * OWN :, :] = jnp.zeros((4, 1, BLK), F32)
    for high in range(2):
        for low in range(2):
            for m in range(3):
                lo = PACK * high + OWN * (2 * m + low)
                packed[2 * high + low, OWN * m : OWN * (m + 1), :] = total[lo : lo + OWN, :]
    out_ref[...] = packed[...].astype(BF16)


def sum_near(parts):
    return pl.pallas_call(
        sum_near_kernel,
        in_specs=[VM],
        out_specs=VM,
        out_shape=shape(4, 40, BLK),
        scratch_shapes=[pltpu.VMEM((2 * PACK, BLK), F32), pltpu.VMEM((4, 40, BLK), F32)],
        compiler_params=params(8),
        name="sum_near",
    )(parts)


def sum_far_kernel(in_ref, out_ref):
    total = jnp.sum(in_ref[...].astype(F32), axis=0)
    for m in range(3):
        out_ref[m] = total[OWN * m : OWN * (m + 1), :]


def sum_far(parts):
    return pl.pallas_call(
        sum_far_kernel,
        in_specs=[VM],
        out_specs=VM,
        out_shape=shape(3, OWN, BLK, dtype=F32),
        compiler_params=params(8),
        name="sum_far",
    )(parts)


def per_device(tokens, grad_out, gate_rows, up_rows, down_rows):
    core = lax.axis_index("c").astype(jnp.int32).reshape(1)
    swap = [(0, 1), (1, 0)]

    def exchange(parts, axes):
        return lax.all_to_all(parts, axes, split_axis=0, concat_axis=0, tiled=True)

    send1, own1, hid = first(core, tokens, grad_out, gate_rows, up_rows, down_rows)
    got1 = lax.ppermute(send1, "c", swap)
    send0, own0 = down(core, hid, grad_out)
    got0 = lax.ppermute(send0, "c", swap)
    parts = add_cores(own0, got0, own1, got1)
    parts = sum_near(exchange(parts, ("y", "zl", "x")))
    return sum_far(exchange(parts, "zh"))


def solution(mesh):
    fine = Mesh(mesh.devices.reshape(4, 4, 2, 2, 4), AXES)
    tok = P(AXES, None)
    return jax.shard_map(
        per_device,
        mesh=fine,
        in_specs=(tok, tok, P(), P(), P()),
        out_specs=P(None, AXES, None),
        check_vma=False,
    )
```

```python
import jax
import jax.numpy as jnp
from jax import lax
from jax.experimental import pallas as pl
from jax.experimental.pallas import tpu as pltpu
from jax.sharding import Mesh, PartitionSpec as P

ROWS = 104
D = 8192
BLK = 256
TOK = 256
NCB = D // BLK
OWN = 13
NR0 = 13
QUART = 104
CUTS = tuple(range(0, D + 1, 1024))
AXES = ("y", "zh", "c", "zl", "x")
TERMS_MIB = 40
F32 = jnp.float32
BF16 = jnp.bfloat16
VM = pl.BlockSpec(memory_space=pltpu.VMEM)
HB = pl.BlockSpec(memory_space=pltpu.HBM)
SM = pl.BlockSpec(memory_space=pltpu.SMEM)


def params(mib):
    return pltpu.CompilerParams(vmem_limit_bytes=mib * 1024 * 1024)


def shape(*dims, dtype=BF16):
    return jax.ShapeDtypeStruct(dims, dtype)


def permuted(term, rows, out, i):
    for half in range(2):
        lanes = slice(128 * half, 128 * (half + 1))
        rows[i, half] = term[:, lanes]
        for r0 in range(NR0):
            out[i, 8 * r0 : 8 * (r0 + 1), lanes] = rows[i, half, pl.ds(r0, 8, stride=NR0), :]


def weight_grads(mine, a_ref, v_ref, send, own, first, count):
    for cb in range(NCB):
        res = jnp.dot(a_ref[...], v_ref[:, cb * BLK : (cb + 1) * BLK], preferred_element_type=F32)
        for r0 in range(NR0):
            quarter, off = divmod(NCB * r0 + cb, QUART)
            out = own if quarter % 2 == mine else send
            for m in range(count):
                lo = m * ROWS + 8 * r0
                out[first + m, QUART * (quarter // 2) + off] = res[lo : lo + 8, :].astype(BF16)


def fetch(pairs, sems):
    copies = []
    for i, (lo, hi) in enumerate(zip(CUTS, CUTS[1:])):
        cols = pl.ds(lo, hi - lo)
        copies.append([pltpu.make_async_copy(s.at[:, cols], d.at[:, cols], sems.at[k, i]) for k, (s, d) in enumerate(pairs)])
        for copy in copies[-1]:
            copy.start()
    return copies


def terms_kernel(c_ref, x_hbm, g_hbm, wg_hbm, wu_hbm, wd_hbm, send, own, *scratch):
    x_ref, g_ref, wg_ref, wu_ref, wd_ref, rows, tmp, a0_ref, a12_ref, sems = scratch
    pairs = ((x_hbm, x_ref), (wg_hbm, wg_ref), (wu_hbm, wu_ref), (g_hbm, g_ref), (wd_hbm, wd_ref))
    fetched = fetch(pairs, sems)

    def project(v, w):
        return lax.dot_general(v, w, (((1,), (1,)), ((), ())), preferred_element_type=F32)

    gate_up = jnp.zeros((TOK, 2 * ROWS), F32)
    dh = jnp.zeros((TOK, ROWS), F32)
    for copies, lo, hi in zip(fetched, CUTS, CUTS[1:]):
        for copy in copies:
            copy.wait()
        cols = slice(lo, hi)
        both = jnp.concatenate([wg_ref[:, cols], wu_ref[:, cols]], axis=0)
        gate_up = gate_up + project(x_ref[:, cols], both)
        dh = dh + project(g_ref[:, cols], wd_ref[:, cols])
    gate_up = gate_up.T
    gate, up, dh = gate_up[:ROWS], gate_up[ROWS:], dh.T
    sig = jax.nn.sigmoid(gate)
    act = gate * sig
    permuted(act * up, rows, tmp, 0)
    permuted(dh * up * sig * (1.0 + gate * (1.0 - sig)), rows, tmp, 1)
    permuted(dh * act, rows, tmp, 2)
    a0_ref[...] = tmp[0].astype(BF16)
    a12_ref[...] = jnp.concatenate([tmp[1], tmp[2]], axis=0).astype(BF16)
    for mine in range(2):

        @pl.when(c_ref[0] == mine)
        def _(mine=mine):
            weight_grads(mine, a0_ref, g_ref, send, own, 0, 1)
            weight_grads(mine, a12_ref, x_ref, send, own, 1, 2)


def terms(core, *inputs):
    half = pltpu.VMEM((3, 2 * QUART, 8, BLK), BF16)
    inputs = [pltpu.with_memory_space_constraint(a, pltpu.HBM) for a in inputs]
    return pl.pallas_call(
        terms_kernel,
        in_specs=[SM, HB, HB, HB, HB, HB],
        out_specs=[VM, VM],
        out_shape=[half, half],
        scratch_shapes=[
            pltpu.VMEM((TOK, D), BF16),
            pltpu.VMEM((TOK, D), BF16),
            pltpu.VMEM((ROWS, D), BF16),
            pltpu.VMEM((ROWS, D), BF16),
            pltpu.VMEM((ROWS, D), BF16),
            pltpu.VMEM((3, 2, ROWS, 128), F32),
            pltpu.VMEM((3, ROWS, TOK), F32),
            pltpu.VMEM((ROWS, TOK), BF16),
            pltpu.VMEM((2 * ROWS, TOK), BF16),
            pltpu.SemaphoreType.DMA((5, len(CUTS) - 1)),
        ],
        compiler_params=params(TERMS_MIB),
        name="terms",
    )(core, *inputs)


def add_kernel(own, got, out_ref, packed):
    for d in range(8):
        for m in range(3):
            for low in range(2):
                for off in range(OWN):
                    at = QUART * low + OWN * d + off
                    tile = own[m, at].astype(F32) + got[m, at].astype(F32)
                    for half in range(2):
                        lo = OWN * (6 * half + 2 * m + low) + off
                        packed[d, pl.ds(lo, 8, stride=12 * OWN), :] = tile[:, 128 * half : 128 * (half + 1)]
        for y in range(4):
            out_ref[8 * y + d] = packed[d, 24 * OWN * y : 24 * OWN * (y + 1), :].astype(BF16)


def add_cores(own, got):
    return pl.pallas_call(
        add_kernel,
        in_specs=[VM] * 2,
        out_specs=VM,
        out_shape=shape(32, 24 * OWN, 128),
        scratch_shapes=[pltpu.VMEM((8, 8 * 12 * OWN, 128), F32)],
        compiler_params=params(16),
        name="add_cores",
    )(own, got)


def sum_near_kernel(in_ref, out_ref, total, packed):
    total[...] = jnp.sum(in_ref[...].astype(F32), axis=0)
    packed[:, 6 * OWN :, :] = jnp.zeros((4, 2, 128), F32)
    for high in range(2):
        for low in range(2):
            for half in range(2):
                for m in range(3):
                    src = OWN * (12 * high + 6 * half + 2 * m + low)
                    dst = OWN * (3 * half + m)
                    packed[2 * high + low, dst : dst + OWN, :] = total[src : src + OWN, :]
    out_ref[...] = packed[...].astype(BF16)


def sum_near(parts):
    return pl.pallas_call(
        sum_near_kernel,
        in_specs=[VM],
        out_specs=VM,
        out_shape=shape(4, 80, 128),
        scratch_shapes=[pltpu.VMEM((24 * OWN, 128), F32), pltpu.VMEM((4, 80, 128), F32)],
        compiler_params=params(8),
        name="sum_near",
    )(parts)


def sum_far_kernel(in_ref, out_ref):
    total = jnp.sum(in_ref[...].astype(F32), axis=0)
    for half in range(2):
        for m in range(3):
            lo = OWN * (3 * half + m)
            out_ref[m, :, 128 * half : 128 * (half + 1)] = total[lo : lo + OWN, :]


def sum_far(parts):
    return pl.pallas_call(
        sum_far_kernel,
        in_specs=[VM],
        out_specs=VM,
        out_shape=shape(3, OWN, BLK, dtype=F32),
        compiler_params=params(8),
        name="sum_far",
    )(parts)


def per_device(tokens, grad_out, gate_rows, up_rows, down_rows):
    core = lax.axis_index("c").astype(jnp.int32).reshape(1)
    swap = [(0, 1), (1, 0)]

    def exchange(parts, axes):
        return lax.all_to_all(parts, axes, split_axis=0, concat_axis=0, tiled=True)

    send, own = terms(core, tokens, grad_out, gate_rows, up_rows, down_rows)
    parts = add_cores(own, lax.ppermute(send, "c", swap))
    parts = sum_near(exchange(parts, ("y", "zl", "x")))
    return sum_far(exchange(parts, "zh"))


def solution(mesh):
    fine = Mesh(mesh.devices.reshape(4, 4, 2, 2, 4), AXES)
    tok = P(AXES, None)
    return jax.shard_map(
        per_device,
        mesh=fine,
        in_specs=(tok, tok, P(), P(), P()),
        out_specs=P(None, AXES, None),
        check_vma=False,
    )
```

```python
import functools

import jax
import jax.numpy as jnp
from jax import lax
from jax.experimental import pallas as pl
from jax.experimental.pallas import tpu as pltpu
from jax.sharding import Mesh, PartitionSpec as P

ROWS = 104
D = 8192
BLK = 256
TOK = 256
NCB = D // BLK
OWN = 13
NR0 = 13
QUART = 104
CUTS = tuple(range(0, D + 1, 1024))
AXES = ("y", "zh", "c", "zl", "x")
PAD = 160
TERMS_MIB = 40
F32 = jnp.float32
BF16 = jnp.bfloat16
VM = pl.BlockSpec(memory_space=pltpu.VMEM)
HB = pl.BlockSpec(memory_space=pltpu.HBM)


def params(mib):
    return pltpu.CompilerParams(vmem_limit_bytes=mib * 1024 * 1024)


def shape(*dims, dtype=BF16):
    return jax.ShapeDtypeStruct(dims, dtype)


def permuted(term, rows, out, i):
    for half in range(2):
        lanes = slice(128 * half, 128 * (half + 1))
        rows[i, half] = term[:, lanes]
        for r0 in range(NR0):
            out[i, 8 * r0 : 8 * (r0 + 1), lanes] = rows[i, half, pl.ds(r0, 8, stride=NR0), :]


def weight_grads(mine, a_ref, v_ref, sends, owns):
    for cb in range(NCB):
        res = jnp.dot(a_ref[...], v_ref[:, cb * BLK : (cb + 1) * BLK], preferred_element_type=F32)
        for r0 in range(NR0):
            quarter, off = divmod(NCB * r0 + cb, QUART)
            for m, out in enumerate(owns if quarter % 2 == mine else sends):
                lo = m * ROWS + 8 * r0
                out[QUART * (quarter // 2) + off] = res[lo : lo + 8, :].astype(BF16)


def fetch(pairs, sems):
    copies = []
    for i, (lo, hi) in enumerate(zip(CUTS, CUTS[1:])):
        cols = pl.ds(lo, hi - lo)
        copies.append([pltpu.make_async_copy(s.at[:, cols], d.at[:, cols], sems.at[k, i]) for k, (s, d) in enumerate(pairs)])
        for copy in copies[-1]:
            copy.start()
    return copies


def terms_kernel(x_hbm, g_hbm, wg_hbm, wu_hbm, wd_hbm, *rest):
    sends, owns, scratch = rest[0:3], rest[3:6], rest[6:]
    x_ref, g_ref, wg_ref, wu_ref, wd_ref, rows, tmp, a0_ref, a12_ref, sems = scratch
    pairs = ((x_hbm, x_ref), (wg_hbm, wg_ref), (wu_hbm, wu_ref), (g_hbm, g_ref), (wd_hbm, wd_ref))
    fetched = fetch(pairs, sems)

    def project(v, w):
        return lax.dot_general(v, w, (((1,), (1,)), ((), ())), preferred_element_type=F32)

    gate_up = jnp.zeros((TOK, 2 * ROWS), F32)
    dh = jnp.zeros((TOK, ROWS), F32)
    for copies, lo, hi in zip(fetched, CUTS, CUTS[1:]):
        for copy in copies:
            copy.wait()
        cols = slice(lo, hi)
        both = jnp.concatenate([wg_ref[:, cols], wu_ref[:, cols]], axis=0)
        gate_up = gate_up + project(x_ref[:, cols], both)
        dh = dh + project(g_ref[:, cols], wd_ref[:, cols])
    gate_up = gate_up.T
    gate, up, dh = gate_up[:ROWS], gate_up[ROWS:], dh.T
    sig = jax.nn.sigmoid(gate)
    act = gate * sig
    permuted(act * up, rows, tmp, 0)
    permuted(dh * up * sig * (1.0 + gate * (1.0 - sig)), rows, tmp, 1)
    permuted(dh * act, rows, tmp, 2)
    a0_ref[...] = tmp[0].astype(BF16)
    a12_ref[...] = jnp.concatenate([tmp[1], tmp[2]], axis=0).astype(BF16)
    for mine in range(2):

        @pl.when(lax.axis_index("c") == mine)
        def _(mine=mine):
            weight_grads(mine, a0_ref, g_ref, sends[:1], owns[:1])
            weight_grads(mine, a12_ref, x_ref, sends[1:], owns[1:])


def terms(*inputs):
    half = pltpu.VMEM((2 * QUART, 8, BLK), BF16)
    inputs = [pltpu.with_memory_space_constraint(a, pltpu.HBM) for a in inputs]
    return pl.pallas_call(
        terms_kernel,
        in_specs=[HB] * 5,
        out_specs=[VM] * 6,
        out_shape=[half] * 6,
        scratch_shapes=[
            pltpu.VMEM((TOK, D), BF16),
            pltpu.VMEM((TOK, D), BF16),
            pltpu.VMEM((ROWS, D), BF16),
            pltpu.VMEM((ROWS, D), BF16),
            pltpu.VMEM((ROWS, D), BF16),
            pltpu.VMEM((3, 2, ROWS, 128), F32),
            pltpu.VMEM((3, ROWS, TOK), F32),
            pltpu.VMEM((ROWS, TOK), BF16),
            pltpu.VMEM((2 * ROWS, TOK), BF16),
            pltpu.SemaphoreType.DMA((5, len(CUTS) - 1)),
        ],
        compiler_params=params(TERMS_MIB),
        name="terms",
    )(*inputs)


def pair_place(axis):
    at = lax.axis_index(axis)
    return at if axis == "zl" else (at >> lax.axis_index("c")) & 1


def add_kernel(axis, own, got, keep, give, halves):
    for d in range(8):
        for low in range(2):
            for off in range(OWN):
                at = QUART * low + OWN * d + off
                tile = own[at].astype(F32) + got[at].astype(F32)
                for half in range(2):
                    lo = OWN * low + off
                    halves[half, d, pl.ds(lo, 8, stride=2 * OWN), :] = tile[:, 128 * half : 128 * (half + 1)]
    mine = pair_place(axis)
    keep[...] = halves[mine].astype(BF16)
    give[...] = halves[1 - mine].astype(BF16)


def add_cores(axis, own, got):
    return pl.pallas_call(
        functools.partial(add_kernel, axis),
        in_specs=[VM] * 2,
        out_specs=[VM] * 2,
        out_shape=[shape(8, 16 * OWN, 128)] * 2,
        scratch_shapes=[pltpu.VMEM((2, 8, 16 * OWN, 128), F32)],
        compiler_params=params(16),
        name="add_" + axis,
    )(own, got)


def add_pair_kernel(k0, k1, k2, g0, g1, g2, out_ref, total, packed):
    n = 4 * OWN
    packed[:, 3 * n :, :] = jnp.zeros((32, PAD - 3 * n, 128), F32)
    for m, (keep, got) in enumerate(((k0, g0), (k1, g1), (k2, g2))):
        total[...] = keep[...].astype(F32) + got[...].astype(F32)
        for d in range(8):
            for y in range(4):
                packed[8 * y + d, n * m : n * (m + 1), :] = total[d, n * y : n * (y + 1), :]
    out_ref[...] = packed[...].astype(BF16)


def add_pair(*parts):
    return pl.pallas_call(
        add_pair_kernel,
        in_specs=[VM] * 6,
        out_specs=VM,
        out_shape=shape(32, PAD, 128),
        scratch_shapes=[pltpu.VMEM((8, 16 * OWN, 128), F32), pltpu.VMEM((32, PAD, 128), F32)],
        compiler_params=params(16),
        name="add_pair",
    )(*parts)


def sum_near_kernel(in_ref, out_ref, total, packed):
    def add(sources, m):
        lo, hi = 4 * OWN * m, 4 * OWN * (m + 1)
        value = in_ref[sources[0], lo:hi, :].astype(F32)
        for source in sources[1:]:
            value = value + in_ref[source, lo:hi, :].astype(F32)
        return value

    for core in range(2):

        @pl.when(lax.axis_index("c") == core)
        def _(core=core):
            for half in range(2):
                total[0, half] = add([s for s in range(32) if (s % 4 >> core) & 1 == half], 0)
                total[1, half] = add([s for s in range(32) if (s // 8 >> core) & 1 == half], 1)

    for half in range(2):
        total[2, half] = add([s for s in range(32) if s // 4 % 2 == half], 2)
    packed[:, 6 * OWN :, :] = jnp.zeros((4, 2, 128), F32)
    for high in range(2):
        for low in range(2):
            for half in range(2):
                for m in range(3):
                    src = OWN * (2 * high + low)
                    dst = OWN * (3 * half + m)
                    packed[2 * high + low, dst : dst + OWN, :] = total[m, half, src : src + OWN, :]
    out_ref[...] = packed[...].astype(BF16)


def sum_near(parts):
    return pl.pallas_call(
        sum_near_kernel,
        in_specs=[VM],
        out_specs=VM,
        out_shape=shape(4, 80, 128),
        scratch_shapes=[pltpu.VMEM((3, 2, 4 * OWN, 128), F32), pltpu.VMEM((4, 80, 128), F32)],
        compiler_params=params(8),
        name="sum_near",
    )(parts)


def sum_far_kernel(in_ref, out_ref):
    total = jnp.sum(in_ref[...].astype(F32), axis=0)
    for half in range(2):
        for m in range(3):
            lo = OWN * (3 * half + m)
            out_ref[m, :, 128 * half : 128 * (half + 1)] = total[lo : lo + OWN, :]


def sum_far(parts):
    return pl.pallas_call(
        sum_far_kernel,
        in_specs=[VM],
        out_specs=VM,
        out_shape=shape(3, OWN, BLK, dtype=F32),
        compiler_params=params(8),
        name="sum_far",
    )(parts)


def per_device(tokens, grad_out, gate_rows, up_rows, down_rows):
    def exchange(parts, axes):
        return lax.all_to_all(parts, axes, split_axis=0, concat_axis=0, tiled=True)

    ring = [(i ^ 1, 3 - i) for i in range(4)]
    long = [(i ^ 1, (i + 1 if i % 2 else i - 1) % 8) for i in range(8)]
    pairs = (
        (("c", "x"), [(4 * c + i, 4 * c + ring[i][c]) for c in range(2) for i in range(4)]),
        (("y", "c"), [(2 * i + c, 2 * ring[i][c] + c) for c in range(2) for i in range(4)]),
        (("zh", "c", "zl"), [(place(i, c), place(long[i][c], c)) for c in range(2) for i in range(8)]),
    )
    sends_owns = terms(tokens, grad_out, gate_rows, up_rows, down_rows)
    keeps, gots = [], []
    for axis, send, own, (axes, perm) in zip(("x", "y", "zl"), sends_owns[:3], sends_owns[3:], pairs, strict=True):
        keep, give = add_cores(axis, own, lax.ppermute(send, "c", [(0, 1), (1, 0)]))
        keeps.append(keep)
        gots.append(lax.ppermute(give, axes, perm))
    parts = sum_near(exchange(add_pair(*keeps, *gots), ("y", "zl", "x")))
    return sum_far(exchange(parts, "zh"))


def place(z, c):
    return 4 * (z // 2) + 2 * c + z % 2


def solution(mesh):
    fine = Mesh(mesh.devices.reshape(4, 4, 2, 2, 4), AXES)
    tok = P(AXES, None)
    return jax.shard_map(
        per_device,
        mesh=fine,
        in_specs=(tok, tok, P(), P(), P()),
        out_specs=P(None, AXES, None),
        check_vma=False,
    )
```

```python
import functools

import jax
import jax.numpy as jnp
from jax import lax
from jax.experimental import pallas as pl
from jax.experimental.pallas import tpu as pltpu
from jax.sharding import Mesh, PartitionSpec as P

ROWS = 104
D = 8192
BLK = 256
TOK = 256
NCB = D // BLK
OWN = 13
NR0 = 13
QUART = 104
CUTS = tuple(range(0, D + 1, 1024))
AXES = ("y", "zh", "c", "zl", "x")
ORDER = "zxy"
PAD = 80
TERMS_MIB = 40
F32 = jnp.float32
BF16 = jnp.bfloat16
VM = pl.BlockSpec(memory_space=pltpu.VMEM)
HB = pl.BlockSpec(memory_space=pltpu.HBM)


def params(mib):
    return pltpu.CompilerParams(vmem_limit_bytes=mib * 1024 * 1024)


def shape(*dims, dtype=BF16):
    return jax.ShapeDtypeStruct(dims, dtype)


def permuted(term, rows, out, i):
    for half in range(2):
        lanes = slice(128 * half, 128 * (half + 1))
        rows[i, half] = term[:, lanes]
        for r0 in range(NR0):
            out[i, 8 * r0 : 8 * (r0 + 1), lanes] = rows[i, half, pl.ds(r0, 8, stride=NR0), :]


def weight_grads(mine, a_ref, v_ref, sends, owns):
    for cb in range(NCB):
        res = jnp.dot(a_ref[...], v_ref[:, cb * BLK : (cb + 1) * BLK], preferred_element_type=F32)
        for r0 in range(NR0):
            quarter, off = divmod(NCB * r0 + cb, QUART)
            for m, out in enumerate(owns if quarter % 2 == mine else sends):
                lo = m * ROWS + 8 * r0
                out[QUART * (quarter // 2) + off] = res[lo : lo + 8, :].astype(BF16)


def fetch(pairs, sems):
    copies = []
    for i, (lo, hi) in enumerate(zip(CUTS, CUTS[1:])):
        cols = pl.ds(lo, hi - lo)
        copies.append([pltpu.make_async_copy(s.at[:, cols], d.at[:, cols], sems.at[k, i]) for k, (s, d) in enumerate(pairs)])
        for copy in copies[-1]:
            copy.start()
    return copies


def terms_kernel(x_hbm, g_hbm, wg_hbm, wu_hbm, wd_hbm, *rest):
    sends, owns, scratch = rest[0:3], rest[3:6], rest[6:]
    x_ref, g_ref, wg_ref, wu_ref, wd_ref, rows, tmp, a0_ref, a12_ref, sems = scratch
    pairs = ((x_hbm, x_ref), (wg_hbm, wg_ref), (wu_hbm, wu_ref), (g_hbm, g_ref), (wd_hbm, wd_ref))
    fetched = fetch(pairs, sems)

    def project(v, w):
        return lax.dot_general(v, w, (((1,), (1,)), ((), ())), preferred_element_type=F32)

    gate_up = jnp.zeros((TOK, 2 * ROWS), F32)
    dh = jnp.zeros((TOK, ROWS), F32)
    for copies, lo, hi in zip(fetched, CUTS, CUTS[1:]):
        for copy in copies:
            copy.wait()
        cols = slice(lo, hi)
        both = jnp.concatenate([wg_ref[:, cols], wu_ref[:, cols]], axis=0)
        gate_up = gate_up + project(x_ref[:, cols], both)
        dh = dh + project(g_ref[:, cols], wd_ref[:, cols])
    gate_up = gate_up.T
    gate, up, dh = gate_up[:ROWS], gate_up[ROWS:], dh.T
    sig = jax.nn.sigmoid(gate)
    act = gate * sig
    permuted(act * up, rows, tmp, 0)
    permuted(dh * up * sig * (1.0 + gate * (1.0 - sig)), rows, tmp, 1)
    permuted(dh * act, rows, tmp, 2)
    a0_ref[...] = tmp[0].astype(BF16)
    a12_ref[...] = jnp.concatenate([tmp[1], tmp[2]], axis=0).astype(BF16)
    for mine in range(2):

        @pl.when(lax.axis_index("c") == mine)
        def _(mine=mine):
            weight_grads(mine, a0_ref, g_ref, sends[:1], owns[:1])
            weight_grads(mine, a12_ref, x_ref, sends[1:], owns[1:])


def terms(*inputs):
    half = pltpu.VMEM((2 * QUART, 8, BLK), BF16)
    inputs = [pltpu.with_memory_space_constraint(a, pltpu.HBM) for a in inputs]
    return pl.pallas_call(
        terms_kernel,
        in_specs=[HB] * 5,
        out_specs=[VM] * 6,
        out_shape=[half] * 6,
        scratch_shapes=[
            pltpu.VMEM((TOK, D), BF16),
            pltpu.VMEM((TOK, D), BF16),
            pltpu.VMEM((ROWS, D), BF16),
            pltpu.VMEM((ROWS, D), BF16),
            pltpu.VMEM((ROWS, D), BF16),
            pltpu.VMEM((3, 2, ROWS, 128), F32),
            pltpu.VMEM((3, ROWS, TOK), F32),
            pltpu.VMEM((ROWS, TOK), BF16),
            pltpu.VMEM((2 * ROWS, TOK), BF16),
            pltpu.SemaphoreType.DMA((5, len(CUTS) - 1)),
        ],
        compiler_params=params(TERMS_MIB),
        name="terms",
    )(*inputs)


def pair_place(axis, level):
    c = lax.axis_index("c")
    if axis == "z":
        low = lax.axis_index("zl")
        return low if level else ((2 * lax.axis_index("zh") + low + 1 - c) >> 1) & 1
    i = lax.axis_index(axis)
    high, low = i >> 1, i & 1
    return jnp.where(c == 0, high, low) if level else high ^ ((1 - c) * low)


def add_kernel(axis, own, got, keep, give, halves):
    for d in range(8):
        for low in range(2):
            for off in range(OWN):
                at = QUART * low + OWN * d + off
                tile = own[at].astype(F32) + got[at].astype(F32)
                for half in range(2):
                    halves[half, low, d, pl.ds(off, 8, stride=OWN), :] = tile[:, 128 * half : 128 * (half + 1)]
    mine = pair_place(axis, 0)
    keep[...] = halves[mine].astype(BF16)
    give[...] = halves[1 - mine].astype(BF16)


def add_cores(axis, own, got):
    return pl.pallas_call(
        functools.partial(add_kernel, axis),
        in_specs=[VM] * 2,
        out_specs=[VM] * 2,
        out_shape=[shape(2, 8, 8 * OWN, 128)] * 2,
        scratch_shapes=[pltpu.VMEM((2, 2, 8, 8 * OWN, 128), F32)],
        compiler_params=params(16),
        name="add_" + axis,
    )(own, got)


def add_pair_kernel(axis, mine, got, keep, give):
    at = pair_place(axis, 1)
    for out, low in ((keep, at), (give, 1 - at)):
        out[...] = (mine[low].astype(F32) + got[low].astype(F32)).astype(BF16)


def add_pair(axis, mine, got):
    return pl.pallas_call(
        functools.partial(add_pair_kernel, axis),
        in_specs=[VM] * 2,
        out_specs=[VM] * 2,
        out_shape=[shape(8, 8 * OWN, 128)] * 2,
        compiler_params=params(16),
        name="add_pair_" + axis,
    )(mine, got)


def add_four_kernel(k0, k1, k2, g0, g1, g2, out_ref, total, packed):
    n = 2 * OWN
    packed[:, 3 * n :, :] = jnp.zeros((32, PAD - 3 * n, 128), F32)
    for m, (keep, got) in enumerate(((k0, g0), (k1, g1), (k2, g2))):
        total[...] = keep[...].astype(F32) + got[...].astype(F32)
        for d in range(8):
            for y in range(4):
                packed[8 * y + d, n * m : n * (m + 1), :] = total[d, n * y : n * (y + 1), :]
    out_ref[...] = packed[...].astype(BF16)


def add_four(*parts):
    return pl.pallas_call(
        add_four_kernel,
        in_specs=[VM] * 6,
        out_specs=VM,
        out_shape=shape(32, PAD, 128),
        scratch_shapes=[pltpu.VMEM((8, 8 * OWN, 128), F32), pltpu.VMEM((32, PAD, 128), F32)],
        compiler_params=params(16),
        name="add_four",
    )(*parts)


def sum_near_kernel(in_ref, out_ref, total, packed):
    n = 2 * OWN

    def add(sources, m):
        value = in_ref[sources[0], n * m : n * (m + 1), :].astype(F32)
        for source in sources[1:]:
            value = value + in_ref[source, n * m : n * (m + 1), :].astype(F32)
        return value

    mx, my, mz = (ORDER.index(axis) for axis in "xyz")
    for core in range(2):

        @pl.when(lax.axis_index("c") == core)
        def _(core=core):
            for i in range(4):
                high, low = i >> 1, i & 1
                half, part = (high, low) if core else (high ^ low, high)
                total[mx, half, part] = add([s for s in range(32) if s % 4 == i], mx)
                total[my, half, part] = add([s for s in range(32) if s // 8 == i], my)

    total[mz] = jnp.zeros((2, 2, n, 128), F32)
    for low in range(2):
        half = ((2 * lax.axis_index("zh") + low + 1 - lax.axis_index("c")) >> 1) & 1
        total[mz, half, low] = add([s for s in range(32) if s // 4 % 2 == low], mz)
    packed[:, 6 * OWN :, :] = jnp.zeros((4, 2, 128), F32)
    for high in range(2):
        for low in range(2):
            for half in range(2):
                for m in range(3):
                    dst = OWN * (3 * half + m)
                    packed[2 * high + low, dst : dst + OWN, :] = total[m, half, low, OWN * high : OWN * (high + 1), :]
    out_ref[...] = packed[...].astype(BF16)


def sum_near(parts):
    return pl.pallas_call(
        sum_near_kernel,
        in_specs=[VM],
        out_specs=VM,
        out_shape=shape(4, 80, 128),
        scratch_shapes=[pltpu.VMEM((3, 2, 2, 2 * OWN, 128), F32), pltpu.VMEM((4, 80, 128), F32)],
        compiler_params=params(8),
        name="sum_near",
    )(parts)


def sum_far_kernel(in_ref, out_ref):
    total = jnp.sum(in_ref[...].astype(F32), axis=0)
    for half in range(2):
        for m in range(3):
            lo = OWN * (3 * half + m)
            out_ref[m, :, 128 * half : 128 * (half + 1)] = total[lo : lo + OWN, :]


def sum_far(parts):
    return pl.pallas_call(
        sum_far_kernel,
        in_specs=[VM],
        out_specs=VM,
        out_shape=shape(3, OWN, BLK, dtype=F32),
        compiler_params=params(8),
        name="sum_far",
    )(parts)


def per_device(tokens, grad_out, gate_rows, up_rows, down_rows):
    def exchange(parts, axes):
        return lax.all_to_all(parts, axes, split_axis=0, concat_axis=0, tiled=True)

    near = [(i ^ 1, 3 - i) for i in range(4)]
    long = [(i ^ 1, (i + 1 if i % 2 else i - 1) % 8) for i in range(8)]

    def pairs(level):
        cores = [(c, c ^ level) for c in range(2)]
        return {
            "x": (("c", "x"), [(4 * c + i, 4 * c + near[i][k]) for c, k in cores for i in range(4)]),
            "y": (("y", "c"), [(2 * i + c, 2 * near[i][k] + c) for c, k in cores for i in range(4)]),
            "z": (("zh", "c", "zl"), [(place(i, c), place(long[i][k], c)) for c, k in cores for i in range(8)]),
        }

    sends_owns = terms(tokens, grad_out, gate_rows, up_rows, down_rows)
    keeps, gots = [], []
    for axis, send, own in zip(ORDER, sends_owns[:3], sends_owns[3:], strict=True):
        parts = add_cores(axis, own, lax.ppermute(send, "c", [(0, 1), (1, 0)]))
        for level in range(2):
            keep, give = parts if level == 0 else add_pair(axis, keep, got)
            got = lax.ppermute(give, *pairs(level)[axis])
        keeps.append(keep)
        gots.append(got)
    parts = sum_near(exchange(add_four(*keeps, *gots), ("y", "zl", "x")))
    return sum_far(exchange(parts, "zh"))


def place(z, c):
    return 4 * (z // 2) + 2 * c + z % 2


def solution(mesh):
    fine = Mesh(mesh.devices.reshape(4, 4, 2, 2, 4), AXES)
    tok = P(AXES, None)
    return jax.shard_map(
        per_device,
        mesh=fine,
        in_specs=(tok, tok, P(), P(), P()),
        out_specs=P(None, AXES, None),
        check_vma=False,
    )
```

```python
import functools

import jax
import jax.numpy as jnp
from jax import lax
from jax.experimental import pallas as pl
from jax.experimental.pallas import tpu as pltpu
from jax.sharding import Mesh, PartitionSpec as P

ROWS = 104
D = 8192
BLK = 256
TOK = 256
NCB = D // BLK
OWN = 13
NR0 = 13
QUART = 104
CUTS = tuple(range(0, D + 1, 1024))
AXES = ("y", "zh", "c", "zl", "x")
ORDER = "zxy"
PAD = 80
FIRST_MIB = 28
F32 = jnp.float32
BF16 = jnp.bfloat16
VM = pl.BlockSpec(memory_space=pltpu.VMEM)
HB = pl.BlockSpec(memory_space=pltpu.HBM)


def params(mib):
    return pltpu.CompilerParams(vmem_limit_bytes=mib * 1024 * 1024)


def shape(*dims, dtype=BF16):
    return jax.ShapeDtypeStruct(dims, dtype)


def permuted(term, rows, out, i):
    for half in range(2):
        lanes = slice(128 * half, 128 * (half + 1))
        rows[i, half] = term[:, lanes]
        for r0 in range(NR0):
            out[i, 8 * r0 : 8 * (r0 + 1), lanes] = rows[i, half, pl.ds(r0, 8, stride=NR0), :]


def weight_grads(a_ref, v_ref, send, own):
    for mine in range(2):

        @pl.when(lax.axis_index("c") == mine)
        def _(mine=mine):
            for cb in range(NCB):
                res = jnp.dot(a_ref[...], v_ref[:, cb * BLK : (cb + 1) * BLK], preferred_element_type=F32)
                for r0 in range(NR0):
                    quarter, off = divmod(NCB * r0 + cb, QUART)
                    out = own if quarter % 2 == mine else send
                    out[QUART * (quarter // 2) + off] = res[8 * r0 : 8 * (r0 + 1), :].astype(BF16)


def fetch(pairs, sems):
    copies = []
    for i, (lo, hi) in enumerate(zip(CUTS, CUTS[1:])):
        cols = pl.ds(lo, hi - lo)
        copies.append([pltpu.make_async_copy(s.at[:, cols], d.at[:, cols], sems.at[k, i]) for k, (s, d) in enumerate(pairs)])
        for copy in copies[-1]:
            copy.start()
    return copies


def first_kernel(x_hbm, g_hbm, wg_hbm, wu_hbm, wd_hbm, send, own, x_ref, a1_ref, a2_ref, *scratch):
    g_ref, wg_ref, wu_ref, wd_ref, rows, tmp, a0_ref, sems = scratch
    pairs = ((x_hbm, x_ref), (wg_hbm, wg_ref), (wu_hbm, wu_ref), (g_hbm, g_ref), (wd_hbm, wd_ref))
    fetched = fetch(pairs, sems)

    def project(v, w):
        return lax.dot_general(v, w, (((1,), (1,)), ((), ())), preferred_element_type=F32)

    gate_up = jnp.zeros((TOK, 2 * ROWS), F32)
    dh = jnp.zeros((TOK, ROWS), F32)
    for copies, lo, hi in zip(fetched, CUTS, CUTS[1:]):
        for copy in copies:
            copy.wait()
        cols = slice(lo, hi)
        both = jnp.concatenate([wg_ref[:, cols], wu_ref[:, cols]], axis=0)
        gate_up = gate_up + project(x_ref[:, cols], both)
        dh = dh + project(g_ref[:, cols], wd_ref[:, cols])
    gate_up = gate_up.T
    gate, up, dh = gate_up[:ROWS], gate_up[ROWS:], dh.T
    sig = jax.nn.sigmoid(gate)
    act = gate * sig
    permuted(act * up, rows, tmp, 0)
    permuted(dh * up * sig * (1.0 + gate * (1.0 - sig)), rows, tmp, 1)
    permuted(dh * act, rows, tmp, 2)
    for i, out in enumerate((a0_ref, a1_ref, a2_ref)):
        out[...] = tmp[i].astype(BF16)
    weight_grads(a0_ref, g_ref, send, own)


def first(*inputs):
    inputs = [pltpu.with_memory_space_constraint(a, pltpu.HBM) for a in inputs]
    half = pltpu.VMEM((2 * QUART, 8, BLK), BF16)
    act = pltpu.VMEM((ROWS, TOK), BF16)
    return pl.pallas_call(
        first_kernel,
        in_specs=[HB] * 5,
        out_specs=[VM] * 5,
        out_shape=[half, half, pltpu.VMEM((TOK, D), BF16), act, act],
        scratch_shapes=[
            pltpu.VMEM((TOK, D), BF16),
            pltpu.VMEM((ROWS, D), BF16),
            pltpu.VMEM((ROWS, D), BF16),
            pltpu.VMEM((ROWS, D), BF16),
            pltpu.VMEM((3, 2, ROWS, 128), F32),
            pltpu.VMEM((3, ROWS, TOK), F32),
            pltpu.VMEM((ROWS, TOK), BF16),
            pltpu.SemaphoreType.DMA((5, len(CUTS) - 1)),
        ],
        compiler_params=params(FIRST_MIB),
        name="first",
    )(*inputs)


def grads(a, v):
    half = pltpu.VMEM((2 * QUART, 8, BLK), BF16)
    return pl.pallas_call(
        weight_grads,
        in_specs=[VM] * 2,
        out_specs=[VM] * 2,
        out_shape=[half] * 2,
        compiler_params=params(16),
        cost_estimate=pl.CostEstimate(flops=2 * ROWS * TOK * D, bytes_accessed=8 * TOK * D, transcendentals=0),
        name="grads",
    )(a, v)


def pair_place(axis, level):
    c = lax.axis_index("c")
    if axis == "z":
        low = lax.axis_index("zl")
        return low if level else ((2 * lax.axis_index("zh") + low + 1 - c) >> 1) & 1
    i = lax.axis_index(axis)
    high, low = i >> 1, i & 1
    return jnp.where(c == 0, high, low) if level else high ^ ((1 - c) * low)


def add_kernel(axis, own, got, keep, give, halves):
    for d in range(8):
        for low in range(2):
            for off in range(OWN):
                at = QUART * low + OWN * d + off
                tile = own[at].astype(F32) + got[at].astype(F32)
                for half in range(2):
                    halves[half, low, d, pl.ds(off, 8, stride=OWN), :] = tile[:, 128 * half : 128 * (half + 1)]
    mine = pair_place(axis, 0)
    keep[...] = halves[mine].astype(BF16)
    give[...] = halves[1 - mine].astype(BF16)


def add_cores(axis, own, got):
    return pl.pallas_call(
        functools.partial(add_kernel, axis),
        in_specs=[VM] * 2,
        out_specs=[VM] * 2,
        out_shape=[shape(2, 8, 8 * OWN, 128)] * 2,
        scratch_shapes=[pltpu.VMEM((2, 2, 8, 8 * OWN, 128), F32)],
        compiler_params=params(16),
        name="add_" + axis,
    )(own, got)


def add_pair_kernel(axis, mine, got, keep, give):
    at = pair_place(axis, 1)
    for out, low in ((keep, at), (give, 1 - at)):
        out[...] = (mine[low].astype(F32) + got[low].astype(F32)).astype(BF16)


def add_pair(axis, mine, got):
    return pl.pallas_call(
        functools.partial(add_pair_kernel, axis),
        in_specs=[VM] * 2,
        out_specs=[VM] * 2,
        out_shape=[shape(8, 8 * OWN, 128)] * 2,
        compiler_params=params(16),
        name="add_pair_" + axis,
    )(mine, got)


def add_four_kernel(k0, k1, k2, g0, g1, g2, out_ref, total, packed):
    n = 2 * OWN
    packed[:, 3 * n :, :] = jnp.zeros((32, PAD - 3 * n, 128), F32)
    for m, (keep, got) in enumerate(((k0, g0), (k1, g1), (k2, g2))):
        total[...] = keep[...].astype(F32) + got[...].astype(F32)
        for d in range(8):
            for y in range(4):
                packed[8 * y + d, n * m : n * (m + 1), :] = total[d, n * y : n * (y + 1), :]
    out_ref[...] = packed[...].astype(BF16)


def add_four(*parts):
    return pl.pallas_call(
        add_four_kernel,
        in_specs=[VM] * 6,
        out_specs=VM,
        out_shape=shape(32, PAD, 128),
        scratch_shapes=[pltpu.VMEM((8, 8 * OWN, 128), F32), pltpu.VMEM((32, PAD, 128), F32)],
        compiler_params=params(16),
        name="add_four",
    )(*parts)


def sum_near_kernel(in_ref, out_ref, total, packed):
    n = 2 * OWN

    def add(sources, m):
        value = in_ref[sources[0], n * m : n * (m + 1), :].astype(F32)
        for source in sources[1:]:
            value = value + in_ref[source, n * m : n * (m + 1), :].astype(F32)
        return value

    mx, my, mz = (ORDER.index(axis) for axis in "xyz")
    for core in range(2):

        @pl.when(lax.axis_index("c") == core)
        def _(core=core):
            for i in range(4):
                high, low = i >> 1, i & 1
                half, part = (high, low) if core else (high ^ low, high)
                total[mx, half, part] = add([s for s in range(32) if s % 4 == i], mx)
                total[my, half, part] = add([s for s in range(32) if s // 8 == i], my)

    total[mz] = jnp.zeros((2, 2, n, 128), F32)
    for low in range(2):
        half = ((2 * lax.axis_index("zh") + low + 1 - lax.axis_index("c")) >> 1) & 1
        total[mz, half, low] = add([s for s in range(32) if s // 4 % 2 == low], mz)
    packed[:, 6 * OWN :, :] = jnp.zeros((4, 2, 128), F32)
    for high in range(2):
        for low in range(2):
            for half in range(2):
                for m in range(3):
                    dst = OWN * (3 * half + m)
                    packed[2 * high + low, dst : dst + OWN, :] = total[m, half, low, OWN * high : OWN * (high + 1), :]
    out_ref[...] = packed[...].astype(BF16)


def sum_near(parts):
    return pl.pallas_call(
        sum_near_kernel,
        in_specs=[VM],
        out_specs=VM,
        out_shape=shape(4, 80, 128),
        scratch_shapes=[pltpu.VMEM((3, 2, 2, 2 * OWN, 128), F32), pltpu.VMEM((4, 80, 128), F32)],
        compiler_params=params(8),
        name="sum_near",
    )(parts)


def sum_far_kernel(in_ref, out_ref):
    total = jnp.sum(in_ref[...].astype(F32), axis=0)
    for half in range(2):
        for m in range(3):
            lo = OWN * (3 * half + m)
            out_ref[m, :, 128 * half : 128 * (half + 1)] = total[lo : lo + OWN, :]


def sum_far(parts):
    return pl.pallas_call(
        sum_far_kernel,
        in_specs=[VM],
        out_specs=VM,
        out_shape=shape(3, OWN, BLK, dtype=F32),
        compiler_params=params(8),
        name="sum_far",
    )(parts)


def per_device(tokens, grad_out, gate_rows, up_rows, down_rows):
    def exchange(parts, axes):
        return lax.all_to_all(parts, axes, split_axis=0, concat_axis=0, tiled=True)

    near = [(i ^ 1, 3 - i) for i in range(4)]
    long = [(i ^ 1, (i + 1 if i % 2 else i - 1) % 8) for i in range(8)]

    def pairs(level):
        cores = [(c, c ^ level) for c in range(2)]
        return {
            "x": (("c", "x"), [(4 * c + i, 4 * c + near[i][k]) for c, k in cores for i in range(4)]),
            "y": (("y", "c"), [(2 * i + c, 2 * near[i][k] + c) for c, k in cores for i in range(4)]),
            "z": (("zh", "c", "zl"), [(place(i, c), place(long[i][k], c)) for c, k in cores for i in range(8)]),
        }

    send, own, x_here, *acts = first(tokens, grad_out, gate_rows, up_rows, down_rows)
    keeps, gots = [], []
    for m, axis in enumerate(ORDER):
        if m:
            send, own = grads(acts[m - 1], x_here)
        parts = add_cores(axis, own, lax.ppermute(send, "c", [(0, 1), (1, 0)]))
        for level in range(2):
            keep, give = parts if level == 0 else add_pair(axis, keep, got)
            got = lax.ppermute(give, *pairs(level)[axis])
        keeps.append(keep)
        gots.append(got)
    parts = sum_near(exchange(add_four(*keeps, *gots), ("y", "zl", "x")))
    return sum_far(exchange(parts, "zh"))


def place(z, c):
    return 4 * (z // 2) + 2 * c + z % 2


def solution(mesh):
    fine = Mesh(mesh.devices.reshape(4, 4, 2, 2, 4), AXES)
    tok = P(AXES, None)
    return jax.shard_map(
        per_device,
        mesh=fine,
        in_specs=(tok, tok, P(), P(), P()),
        out_specs=P(None, AXES, None),
        check_vma=False,
    )
```

```python
import functools

import jax
import jax.numpy as jnp
from jax import lax
from jax.experimental import pallas as pl
from jax.experimental.pallas import tpu as pltpu
from jax.sharding import Mesh, PartitionSpec as P

ROWS = 104
D = 8192
BLK = 256
TOK = 256
NCB = D // BLK
OWN = 13
NR0 = 13
QUART = 104
CUTS = tuple(range(0, D + 1, 1024))
AXES = ("y", "zh", "c", "zl", "x")
ORDER = "zxy"
PAD = 80
FIRST_MIB = 28
F32 = jnp.float32
BF16 = jnp.bfloat16
VM = pl.BlockSpec(memory_space=pltpu.VMEM)
HB = pl.BlockSpec(memory_space=pltpu.HBM)


def params(mib):
    return pltpu.CompilerParams(vmem_limit_bytes=mib * 1024 * 1024)


def shape(*dims, dtype=BF16):
    return jax.ShapeDtypeStruct(dims, dtype)


def permuted(term, rows, out, i):
    for half in range(2):
        lanes = slice(128 * half, 128 * (half + 1))
        rows[i, half] = term[:, lanes]
        for r0 in range(NR0):
            out[i, 8 * r0 : 8 * (r0 + 1), lanes] = rows[i, half, pl.ds(r0, 8, stride=NR0), :]


def weight_grads(a_ref, v_ref, send, own):
    for mine in range(2):

        @pl.when(lax.axis_index("c") == mine)
        def _(mine=mine):
            for cb in range(NCB):
                res = jnp.dot(a_ref[...], v_ref[:, cb * BLK : (cb + 1) * BLK], preferred_element_type=F32)
                for r0 in range(NR0):
                    quarter, off = divmod(NCB * r0 + cb, QUART)
                    out = own if quarter % 2 == mine else send
                    out[QUART * (quarter // 2) + off] = res[8 * r0 : 8 * (r0 + 1), :].astype(BF16)


def fetch(pairs, sems):
    copies = []
    for i, (lo, hi) in enumerate(zip(CUTS, CUTS[1:])):
        cols = pl.ds(lo, hi - lo)
        copies.append([pltpu.make_async_copy(s.at[:, cols], d.at[:, cols], sems.at[k, i]) for k, (s, d) in enumerate(pairs)])
        for copy in copies[-1]:
            copy.start()
    return copies


def first_kernel(x_hbm, g_hbm, wg_hbm, wu_hbm, wd_hbm, send, own, x_ref, a1_ref, a2_ref, *scratch):
    g_ref, wg_ref, wu_ref, wd_ref, rows, tmp, a0_ref, sems = scratch
    pairs = ((x_hbm, x_ref), (wg_hbm, wg_ref), (wu_hbm, wu_ref), (g_hbm, g_ref), (wd_hbm, wd_ref))
    fetched = fetch(pairs, sems)

    def project(v, w):
        return lax.dot_general(v, w, (((1,), (1,)), ((), ())), preferred_element_type=F32)

    gate_up = jnp.zeros((TOK, 2 * ROWS), F32)
    dh = jnp.zeros((TOK, ROWS), F32)
    for copies, lo, hi in zip(fetched, CUTS, CUTS[1:]):
        for copy in copies:
            copy.wait()
        cols = slice(lo, hi)
        both = jnp.concatenate([wg_ref[:, cols], wu_ref[:, cols]], axis=0)
        gate_up = gate_up + project(x_ref[:, cols], both)
        dh = dh + project(g_ref[:, cols], wd_ref[:, cols])
    gate_up = gate_up.T
    gate, up, dh = gate_up[:ROWS], gate_up[ROWS:], dh.T
    sig = jax.nn.sigmoid(gate)
    act = gate * sig
    permuted(act * up, rows, tmp, 0)
    permuted(dh * up * sig * (1.0 + gate * (1.0 - sig)), rows, tmp, 1)
    permuted(dh * act, rows, tmp, 2)
    for i, out in enumerate((a0_ref, a1_ref, a2_ref)):
        out[...] = tmp[i].astype(BF16)
    weight_grads(a0_ref, g_ref, send, own)


def first(*inputs):
    inputs = [pltpu.with_memory_space_constraint(a, pltpu.HBM) for a in inputs]
    half = pltpu.VMEM((2 * QUART, 8, BLK), BF16)
    act = pltpu.VMEM((ROWS, TOK), BF16)
    return pl.pallas_call(
        first_kernel,
        in_specs=[HB] * 5,
        out_specs=[VM] * 5,
        out_shape=[half, half, pltpu.VMEM((TOK, D), BF16), act, act],
        scratch_shapes=[
            pltpu.VMEM((TOK, D), BF16),
            pltpu.VMEM((ROWS, D), BF16),
            pltpu.VMEM((ROWS, D), BF16),
            pltpu.VMEM((ROWS, D), BF16),
            pltpu.VMEM((3, 2, ROWS, 128), F32),
            pltpu.VMEM((3, ROWS, TOK), F32),
            pltpu.VMEM((ROWS, TOK), BF16),
            pltpu.SemaphoreType.DMA((5, len(CUTS) - 1)),
        ],
        compiler_params=params(FIRST_MIB),
        name="first",
    )(*inputs)


def grads(a, v):
    half = pltpu.VMEM((2 * QUART, 8, BLK), BF16)
    return pl.pallas_call(
        weight_grads,
        in_specs=[VM] * 2,
        out_specs=[VM] * 2,
        out_shape=[half] * 2,
        compiler_params=params(16),
        cost_estimate=pl.CostEstimate(flops=2 * ROWS * TOK * D, bytes_accessed=8 * TOK * D, transcendentals=0),
        name="grads",
    )(a, v)


def pair_place(axis, level):
    c = lax.axis_index("c")
    if axis == "z":
        low = lax.axis_index("zl")
        return low if level else ((2 * lax.axis_index("zh") + low + 1 - c) >> 1) & 1
    i = lax.axis_index(axis)
    high, low = i >> 1, i & 1
    return jnp.where(c == 0, high, low) if level else high ^ ((1 - c) * low)


def add_kernel(axis, own, got, keep, give, halves):
    for d in range(8):
        for low in range(2):
            for off in range(OWN):
                at = QUART * low + OWN * d + off
                tile = own[at].astype(F32) + got[at].astype(F32)
                for half in range(2):
                    halves[half, low, d, pl.ds(off, 8, stride=OWN), :] = tile[:, 128 * half : 128 * (half + 1)]
    mine = pair_place(axis, 0)
    for out, half in ((keep, mine), (give, 1 - mine)):
        out[...] = halves[half].reshape(2, 64 * OWN, 128).astype(BF16)


def add_cores(axis, own, got):
    return pl.pallas_call(
        functools.partial(add_kernel, axis),
        in_specs=[VM] * 2,
        out_specs=[VM] * 2,
        out_shape=[shape(2, 64 * OWN, 128)] * 2,
        scratch_shapes=[pltpu.VMEM((2, 2, 8, 8 * OWN, 128), F32)],
        compiler_params=params(16),
        name="add_" + axis,
    )(own, got)


def add_pair_kernel(axis, mine, got, keep, give):
    at = pair_place(axis, 1)
    for out, low in ((keep, at), (give, 1 - at)):
        out[...] = (mine[low].astype(F32) + got[low].astype(F32)).astype(BF16)


def add_pair(axis, mine, got):
    return pl.pallas_call(
        functools.partial(add_pair_kernel, axis),
        in_specs=[VM] * 2,
        out_specs=[VM] * 2,
        out_shape=[shape(64 * OWN, 128)] * 2,
        compiler_params=params(16),
        name="add_pair_" + axis,
    )(mine, got)


def add_four_kernel(k0, k1, k2, g0, g1, g2, out_ref, total, packed):
    n = 2 * OWN
    packed[:, 3 * n :, :] = jnp.zeros((32, PAD - 3 * n, 128), F32)
    for m, (keep, got) in enumerate(((k0, g0), (k1, g1), (k2, g2))):
        total[...] = (keep[...].astype(F32) + got[...].astype(F32)).reshape(8, 8 * OWN, 128)
        for d in range(8):
            for y in range(4):
                packed[8 * y + d, n * m : n * (m + 1), :] = total[d, n * y : n * (y + 1), :]
    out_ref[...] = packed[...].astype(BF16)


def add_four(*parts):
    return pl.pallas_call(
        add_four_kernel,
        in_specs=[VM] * 6,
        out_specs=VM,
        out_shape=shape(32, PAD, 128),
        scratch_shapes=[pltpu.VMEM((8, 8 * OWN, 128), F32), pltpu.VMEM((32, PAD, 128), F32)],
        compiler_params=params(16),
        name="add_four",
    )(*parts)


def sum_near_kernel(in_ref, out_ref, total, packed):
    n = 2 * OWN

    def add(sources, m):
        value = in_ref[sources[0], n * m : n * (m + 1), :].astype(F32)
        for source in sources[1:]:
            value = value + in_ref[source, n * m : n * (m + 1), :].astype(F32)
        return value

    mx, my, mz = (ORDER.index(axis) for axis in "xyz")
    for core in range(2):

        @pl.when(lax.axis_index("c") == core)
        def _(core=core):
            for i in range(4):
                high, low = i >> 1, i & 1
                half, part = (high, low) if core else (high ^ low, high)
                total[mx, half, part, 0:n] = add([s for s in range(32) if s % 4 == i], mx)
                total[my, half, part, 0:n] = add([s for s in range(32) if s // 8 == i], my)

    total[mz] = jnp.zeros((2, 2, 32, 128), F32)
    for low in range(2):
        half = ((2 * lax.axis_index("zh") + low + 1 - lax.axis_index("c")) >> 1) & 1
        total[mz, half, low, 0:n] = add([s for s in range(32) if s // 4 % 2 == low], mz)
    packed[:, 6 * OWN :, :] = jnp.zeros((4, 2, 128), F32)
    for high in range(2):
        for low in range(2):
            for half in range(2):
                for m in range(3):
                    dst = OWN * (3 * half + m)
                    packed[2 * high + low, dst : dst + OWN, :] = total[m, half, low, OWN * high : OWN * (high + 1), :]
    out_ref[...] = packed[...].astype(BF16)


def sum_near(parts):
    return pl.pallas_call(
        sum_near_kernel,
        in_specs=[VM],
        out_specs=VM,
        out_shape=shape(4, 80, 128),
        scratch_shapes=[pltpu.VMEM((3, 2, 2, 32, 128), F32), pltpu.VMEM((4, 80, 128), F32)],
        compiler_params=params(8),
        name="sum_near",
    )(parts)


def sum_far_kernel(in_ref, out_ref):
    total = jnp.sum(in_ref[...].astype(F32), axis=0)
    for half in range(2):
        for m in range(3):
            lo = OWN * (3 * half + m)
            out_ref[m, :, 128 * half : 128 * (half + 1)] = total[lo : lo + OWN, :]


def sum_far(parts):
    return pl.pallas_call(
        sum_far_kernel,
        in_specs=[VM],
        out_specs=VM,
        out_shape=shape(3, OWN, BLK, dtype=F32),
        compiler_params=params(8),
        name="sum_far",
    )(parts)


def per_device(tokens, grad_out, gate_rows, up_rows, down_rows):
    def exchange(parts, axes):
        return lax.all_to_all(parts, axes, split_axis=0, concat_axis=0, tiled=True)

    near = [(i ^ 1, 3 - i) for i in range(4)]
    long = [(i ^ 1, (i + 1 if i % 2 else i - 1) % 8) for i in range(8)]

    def pairs(level):
        cores = [(c, c ^ level) for c in range(2)]
        return {
            "x": (("c", "x"), [(4 * c + i, 4 * c + near[i][k]) for c, k in cores for i in range(4)]),
            "y": (("y", "c"), [(2 * i + c, 2 * near[i][k] + c) for c, k in cores for i in range(4)]),
            "z": (("zh", "c", "zl"), [(place(i, c), place(long[i][k], c)) for c, k in cores for i in range(8)]),
        }

    send, own, x_here, *acts = first(tokens, grad_out, gate_rows, up_rows, down_rows)
    keeps, gots = [], []
    for m, axis in enumerate(ORDER):
        if m:
            send, own = grads(acts[m - 1], x_here)
        parts = add_cores(axis, own, lax.ppermute(send, "c", [(0, 1), (1, 0)]))
        for level in range(2):
            keep, give = parts if level == 0 else add_pair(axis, keep, got)
            got = lax.ppermute(give, *pairs(level)[axis])
        keeps.append(keep)
        gots.append(got)
    parts = sum_near(exchange(add_four(*keeps, *gots), ("y", "zl", "x")))
    return sum_far(exchange(parts, "zh"))


def place(z, c):
    return 4 * (z // 2) + 2 * c + z % 2


def solution(mesh):
    fine = Mesh(mesh.devices.reshape(4, 4, 2, 2, 4), AXES)
    tok = P(AXES, None)
    return jax.shard_map(
        per_device,
        mesh=fine,
        in_specs=(tok, tok, P(), P(), P()),
        out_specs=P(None, AXES, None),
        check_vma=False,
    )
```

```python
import functools

import jax
import jax.numpy as jnp
from jax import lax
from jax.experimental import pallas as pl
from jax.experimental.pallas import tpu as pltpu
from jax.sharding import Mesh, PartitionSpec as P

ROWS = 104
D = 8192
BLK = 256
TOK = 256
NCB = D // BLK
OWN = 13
NR0 = 13
QUART = 104
CUTS = tuple(range(0, D + 1, 1024))
AXES = ("y", "zh", "c", "zl", "x")
ORDER = "zxy"
PAD = 80
FIRST_MIB = 28
F32 = jnp.float32
BF16 = jnp.bfloat16
VM = pl.BlockSpec(memory_space=pltpu.VMEM)
HB = pl.BlockSpec(memory_space=pltpu.HBM)


def params(mib):
    return pltpu.CompilerParams(vmem_limit_bytes=mib * 1024 * 1024)


def shape(*dims, dtype=BF16):
    return jax.ShapeDtypeStruct(dims, dtype)


def permuted(term, rows, out, i):
    for half in range(2):
        lanes = slice(128 * half, 128 * (half + 1))
        rows[i, half] = term[:, lanes]
        for r0 in range(NR0):
            out[i, 8 * r0 : 8 * (r0 + 1), lanes] = rows[i, half, pl.ds(r0, 8, stride=NR0), :]


def weight_grads(a_ref, v_ref, send, own):
    for mine in range(2):

        @pl.when(lax.axis_index("c") == mine)
        def _(mine=mine):
            for cb in range(NCB):
                res = jnp.dot(a_ref[...], v_ref[:, cb * BLK : (cb + 1) * BLK], preferred_element_type=F32)
                for r0 in range(NR0):
                    quarter, off = divmod(NCB * r0 + cb, QUART)
                    out = own if quarter % 2 == mine else send
                    out[QUART * (quarter // 2) + off] = res[8 * r0 : 8 * (r0 + 1), :].astype(BF16)


def fetch(pairs, sems):
    copies = []
    for i, (lo, hi) in enumerate(zip(CUTS, CUTS[1:])):
        cols = pl.ds(lo, hi - lo)
        copies.append([pltpu.make_async_copy(s.at[:, cols], d.at[:, cols], sems.at[k, i]) for k, (s, d) in enumerate(pairs)])
        for copy in copies[-1]:
            copy.start()
    return copies


def first_kernel(x_hbm, g_hbm, wg_hbm, wu_hbm, wd_hbm, send, own, x_ref, a1_ref, a2_ref, *scratch):
    g_ref, wg_ref, wu_ref, wd_ref, rows, tmp, a0_ref, sems = scratch
    pairs = ((x_hbm, x_ref), (wg_hbm, wg_ref), (wu_hbm, wu_ref), (g_hbm, g_ref), (wd_hbm, wd_ref))
    fetched = fetch(pairs, sems)

    def project(v, w):
        return lax.dot_general(v, w, (((1,), (1,)), ((), ())), preferred_element_type=F32)

    gate_up = jnp.zeros((TOK, 2 * ROWS), F32)
    dh = jnp.zeros((TOK, ROWS), F32)
    for copies, lo, hi in zip(fetched, CUTS, CUTS[1:]):
        early = 3 if hi == D else 5
        for copy in copies[:early]:
            copy.wait()
        cols = slice(lo, hi)
        both = jnp.concatenate([wg_ref[:, cols], wu_ref[:, cols]], axis=0)
        gate_up = gate_up + project(x_ref[:, cols], both)
        for copy in copies[early:]:
            copy.wait()
        dh = dh + project(g_ref[:, cols], wd_ref[:, cols])
    gate_up = gate_up.T
    gate, up, dh = gate_up[:ROWS], gate_up[ROWS:], dh.T
    sig = jax.nn.sigmoid(gate)
    act = gate * sig
    permuted(act * up, rows, tmp, 0)
    permuted(dh * up * sig * (1.0 + gate * (1.0 - sig)), rows, tmp, 1)
    permuted(dh * act, rows, tmp, 2)
    for i, out in enumerate((a0_ref, a1_ref, a2_ref)):
        out[...] = tmp[i].astype(BF16)
    weight_grads(a0_ref, g_ref, send, own)


def first(*inputs):
    inputs = [pltpu.with_memory_space_constraint(a, pltpu.HBM) for a in inputs]
    half = pltpu.VMEM((2 * QUART, 8, BLK), BF16)
    act = pltpu.VMEM((ROWS, TOK), BF16)
    return pl.pallas_call(
        first_kernel,
        in_specs=[HB] * 5,
        out_specs=[VM] * 5,
        out_shape=[half, half, pltpu.VMEM((TOK, D), BF16), act, act],
        scratch_shapes=[
            pltpu.VMEM((TOK, D), BF16),
            pltpu.VMEM((ROWS, D), BF16),
            pltpu.VMEM((ROWS, D), BF16),
            pltpu.VMEM((ROWS, D), BF16),
            pltpu.VMEM((3, 2, ROWS, 128), F32),
            pltpu.VMEM((3, ROWS, TOK), F32),
            pltpu.VMEM((ROWS, TOK), BF16),
            pltpu.SemaphoreType.DMA((5, len(CUTS) - 1)),
        ],
        compiler_params=params(FIRST_MIB),
        name="first",
    )(*inputs)


def grads(a, v):
    half = pltpu.VMEM((2 * QUART, 8, BLK), BF16)
    return pl.pallas_call(
        weight_grads,
        in_specs=[VM] * 2,
        out_specs=[VM] * 2,
        out_shape=[half] * 2,
        compiler_params=params(16),
        cost_estimate=pl.CostEstimate(flops=2 * ROWS * TOK * D, bytes_accessed=8 * TOK * D, transcendentals=0),
        name="grads",
    )(a, v)


def pair_place(axis, level):
    c = lax.axis_index("c")
    if axis == "z":
        low = lax.axis_index("zl")
        return low if level else ((2 * lax.axis_index("zh") + low + 1 - c) >> 1) & 1
    i = lax.axis_index(axis)
    high, low = i >> 1, i & 1
    return jnp.where(c == 0, high, low) if level else high ^ ((1 - c) * low)


def add_kernel(axis, own, got, keep, give, halves):
    for d in range(8):
        for low in range(2):
            for off in range(OWN):
                at = QUART * low + OWN * d + off
                tile = own[at].astype(F32) + got[at].astype(F32)
                for half in range(2):
                    halves[half, low, d, pl.ds(off, 8, stride=OWN), :] = tile[:, 128 * half : 128 * (half + 1)]
    mine = pair_place(axis, 0)
    for out, half in ((keep, mine), (give, 1 - mine)):
        out[...] = halves[half].reshape(2, 64 * OWN, 128).astype(BF16)


def add_cores(axis, own, got):
    return pl.pallas_call(
        functools.partial(add_kernel, axis),
        in_specs=[VM] * 2,
        out_specs=[VM] * 2,
        out_shape=[shape(2, 64 * OWN, 128)] * 2,
        scratch_shapes=[pltpu.VMEM((2, 2, 8, 8 * OWN, 128), F32)],
        compiler_params=params(16),
        name="add_" + axis,
    )(own, got)


def add_pair_kernel(axis, mine, got, keep, give):
    at = pair_place(axis, 1)
    for out, low in ((keep, at), (give, 1 - at)):
        out[...] = (mine[low].astype(F32) + got[low].astype(F32)).astype(BF16)


def add_pair(axis, mine, got):
    return pl.pallas_call(
        functools.partial(add_pair_kernel, axis),
        in_specs=[VM] * 2,
        out_specs=[VM] * 2,
        out_shape=[shape(64 * OWN, 128)] * 2,
        compiler_params=params(16),
        name="add_pair_" + axis,
    )(mine, got)


def add_four_kernel(k0, k1, k2, g0, g1, g2, out_ref, total, packed):
    n = 2 * OWN
    packed[:, 3 * n :, :] = jnp.zeros((32, PAD - 3 * n, 128), F32)
    for m, (keep, got) in enumerate(((k0, g0), (k1, g1), (k2, g2))):
        total[...] = (keep[...].astype(F32) + got[...].astype(F32)).reshape(8, 8 * OWN, 128)
        for d in range(8):
            for y in range(4):
                packed[8 * y + d, n * m : n * (m + 1), :] = total[d, n * y : n * (y + 1), :]
    out_ref[...] = packed[...].astype(BF16)


def add_four(*parts):
    return pl.pallas_call(
        add_four_kernel,
        in_specs=[VM] * 6,
        out_specs=VM,
        out_shape=shape(32, PAD, 128),
        scratch_shapes=[pltpu.VMEM((8, 8 * OWN, 128), F32), pltpu.VMEM((32, PAD, 128), F32)],
        compiler_params=params(16),
        name="add_four",
    )(*parts)


def sum_near_kernel(in_ref, out_ref, total, packed):
    n = 2 * OWN

    def add(sources, m):
        value = in_ref[sources[0], n * m : n * (m + 1), :].astype(F32)
        for source in sources[1:]:
            value = value + in_ref[source, n * m : n * (m + 1), :].astype(F32)
        return value

    mx, my, mz = (ORDER.index(axis) for axis in "xyz")
    for core in range(2):

        @pl.when(lax.axis_index("c") == core)
        def _(core=core):
            for i in range(4):
                high, low = i >> 1, i & 1
                half, part = (high, low) if core else (high ^ low, high)
                total[mx, half, part, 0:n] = add([s for s in range(32) if s % 4 == i], mx)
                total[my, half, part, 0:n] = add([s for s in range(32) if s // 8 == i], my)

    total[mz] = jnp.zeros((2, 2, 32, 128), F32)
    for low in range(2):
        half = ((2 * lax.axis_index("zh") + low + 1 - lax.axis_index("c")) >> 1) & 1
        total[mz, half, low, 0:n] = add([s for s in range(32) if s // 4 % 2 == low], mz)
    packed[:, 6 * OWN :, :] = jnp.zeros((4, 2, 128), F32)
    for high in range(2):
        for low in range(2):
            for half in range(2):
                for m in range(3):
                    dst = OWN * (3 * half + m)
                    packed[2 * high + low, dst : dst + OWN, :] = total[m, half, low, OWN * high : OWN * (high + 1), :]
    out_ref[...] = packed[...].astype(BF16)


def sum_near(parts):
    return pl.pallas_call(
        sum_near_kernel,
        in_specs=[VM],
        out_specs=VM,
        out_shape=shape(4, 80, 128),
        scratch_shapes=[pltpu.VMEM((3, 2, 2, 32, 128), F32), pltpu.VMEM((4, 80, 128), F32)],
        compiler_params=params(8),
        name="sum_near",
    )(parts)


def sum_far_kernel(in_ref, out_ref):
    total = jnp.sum(in_ref[...].astype(F32), axis=0)
    for half in range(2):
        for m in range(3):
            lo = OWN * (3 * half + m)
            out_ref[m, :, 128 * half : 128 * (half + 1)] = total[lo : lo + OWN, :]


def sum_far(parts):
    return pl.pallas_call(
        sum_far_kernel,
        in_specs=[VM],
        out_specs=VM,
        out_shape=shape(3, OWN, BLK, dtype=F32),
        compiler_params=params(8),
        name="sum_far",
    )(parts)


def per_device(tokens, grad_out, gate_rows, up_rows, down_rows):
    def exchange(parts, axes):
        return lax.all_to_all(parts, axes, split_axis=0, concat_axis=0, tiled=True)

    near = [(i ^ 1, 3 - i) for i in range(4)]
    long = [(i ^ 1, (i + 1 if i % 2 else i - 1) % 8) for i in range(8)]

    def pairs(level):
        cores = [(c, c ^ level) for c in range(2)]
        return {
            "x": (("c", "x"), [(4 * c + i, 4 * c + near[i][k]) for c, k in cores for i in range(4)]),
            "y": (("y", "c"), [(2 * i + c, 2 * near[i][k] + c) for c, k in cores for i in range(4)]),
            "z": (("zh", "c", "zl"), [(place(i, c), place(long[i][k], c)) for c, k in cores for i in range(8)]),
        }

    send, own, x_here, *acts = first(tokens, grad_out, gate_rows, up_rows, down_rows)
    keeps, gots = [], []
    for m, axis in enumerate(ORDER):
        if m:
            send, own = grads(acts[m - 1], x_here)
        parts = add_cores(axis, own, lax.ppermute(send, "c", [(0, 1), (1, 0)]))
        for level in range(2):
            keep, give = parts if level == 0 else add_pair(axis, keep, got)
            got = lax.ppermute(give, *pairs(level)[axis])
        keeps.append(keep)
        gots.append(got)
    parts = sum_near(exchange(add_four(*keeps, *gots), ("y", "zl", "x")))
    return sum_far(exchange(parts, "zh"))


def place(z, c):
    return 4 * (z // 2) + 2 * c + z % 2


def solution(mesh):
    fine = Mesh(mesh.devices.reshape(4, 4, 2, 2, 4), AXES)
    tok = P(AXES, None)
    return jax.shard_map(
        per_device,
        mesh=fine,
        in_specs=(tok, tok, P(), P(), P()),
        out_specs=P(None, AXES, None),
        check_vma=False,
    )
```
